128 devices in a mesh: section: 2 (over core), row: 4 (over x), col: 16 (over z, y).
Axes of the slice: x: 4, y: 4, z: 4, core: 2. Of those that a mesh axis runs over, the one named last changes fastest.
Arguments:
- tokens: float32 [2, 4096, 1024], P(None, ('row', 'col')), may hold values from -6 to 6
- cotangent: float32 [2, 4096, 1024], P(None, ('row', 'col')), may hold values from -6 to 6
- seq_lengths: int32 [2, 4], replicated, may hold values from 1 to 2048, 4096 in all within a row
- attention_in: bfloat16 [2, 1024, 3072], P('section', 'row', 'col'), may hold values from -0.1875 to 0.1875
- attention_in_bias: float32 [2, 3072], P('section', 'col'), may hold values from -4 to 4
- attention_out: bfloat16 [2, 1024, 1024], P('section', 'col', 'row'), may hold values from -1.5 to 1.5
- expand_weight: bfloat16 [2, 1024, 4096], P('section', 'row', 'col'), may hold values from -0.1875 to 0.1875
- expand_bias: float32 [2, 4096], P('section', 'col'), may hold values from -4 to 4
- shrink_weight: bfloat16 [2, 4096, 1024], P('section', 'col', 'row'), may hold values from -0.09375 to 0.09375
- output_bias: float32 [2, 1024], P('section'), may hold values from -4 to 4
- attend_gain: float32 [2, 1024], P('section'), may hold values from 0.5 to 1.5
- attend_shift: float32 [2, 1024], P('section'), may hold values from -4 to 4
- feed_gain: float32 [2, 1024], P('section'), may hold values from 0.5 to 1.5
- feed_shift: float32 [2, 1024], P('section'), may hold values from -4 to 4
Outputs:
- layer_outputs: float32 [2, 2, 4096, 1024], P('section', None, ('row', 'col'))
- input_grads: float32 [2, 2, 4096, 1024], P('section', None, ('row', 'col'))
- attention_in_grad: float32 [2, 1024, 3072], P('section', 'row', 'col')
- attention_in_bias_grad: float32 [2, 3072], P('section', 'col')
- attention_out_grad: float32 [2, 1024, 1024], P('section', 'col', 'row')
- expand_weight_grad: float32 [2, 1024, 4096], P('section', 'row', 'col')
- expand_bias_grad: float32 [2, 4096], P('section', 'col')
- shrink_weight_grad: float32 [2, 4096, 1024], P('section', 'col', 'row')
- output_bias_grad: float32 [2, 1024], P('section')
- attend_gain_grad: float32 [2, 1024], P('section')
- attend_shift_grad: float32 [2, 1024], P('section')
- feed_gain_grad: float32 [2, 1024], P('section')
- feed_shift_grad: float32 [2, 1024], P('section')
The draws below stay inside these ranges and needn't reach their ends.
Inputs may be any that keep to these rules, and one draw needn't show every extreme that they name: `seq_lengths`: row m lists the lengths of micro-batch m's sequences in token order; each row sums to 4096 and its largest entry is 2048.
All inputs are finite; a program needn't handle non-finite values.
Results may differ from the reference program's by a relative error of at most 0.03.
Values may be sent and summed in bfloat16 or wider, within the bound.
No kernel may reach another device: no remote copies, remote signals or barrier semaphores. Data moves between devices by JAX's collectives and lax.ppermute only.
A program may use at most 192 MiB of HBM per device.

```python
import math
import jax
import jax.numpy as jnp
import numpy as np
from jax import lax

D = 1024
H = 16
FF = 4096
HD = 64
ROT = 16
M = 2
SEQS = 4
T_MB = 4096
LONGEST = 2048


def shard_levels(own_key, dims, cuts, least, largest):
    gain, own = 1.0, jax.random.fold_in(own_key, 6)
    for dim, blocks in cuts:
        steps = jnp.exp(jax.random.uniform(jax.random.fold_in(own, dim), (blocks,), jnp.float32, least / len(cuts), largest / len(cuts)))
        gain = gain * jnp.repeat(steps, dims[dim] // blocks).reshape([-1 if axis == dim else 1 for axis in range(len(dims))])
    return gain


def profile(count, total, limit, skew):
    portions = [(1 << 20) // math.isqrt(standing ** skew) + 1 for standing in range(2, count + 1)]
    spare, counts = total - limit - (count - 1), [1] * (count - 1)
    while spare > 0:
        free = [i for i in range(count - 1) if counts[i] < limit]
        mass, left = sum([portions[i] for i in free]), spare
        for i in free:
            extra = min(limit - counts[i], max(1, left * portions[i] // mass), spare)
            counts[i] = counts[i] + extra
            spare = spare - extra
    return np.array([limit] + counts)


def uneven_parts(own_key, amount, total, limit, slope):
    if amount == 2:
        one = jax.random.randint(own_key, (), max(1, total - limit), min(limit, total - 1) + 1)
        return jnp.stack([one, total - one])
    sizes = jnp.asarray(profile(amount, total, limit, slope), jnp.int32)
    pairs = (amount - 1) // 2
    donor, sink = sizes[1:1 + 2 * pairs:2], sizes[2:2 + 2 * pairs:2]
    slack = jnp.minimum(donor - 1, limit - sink)
    shifted = jax.random.randint(jax.random.fold_in(own_key, 1), (pairs,), 0, 1 << 20) % (slack + 1)
    sizes = sizes.at[1:1 + 2 * pairs:2].set(donor - shifted).at[2:2 + 2 * pairs:2].set(sink + shifted)
    return sizes[jax.random.permutation(jax.random.fold_in(own_key, 2), amount)]


def gaussian(stream_key, extent, deviation, bound, cuts=(), held_as=jnp.bfloat16):
    values = deviation * jax.random.normal(stream_key, extent, jnp.float32)
    if cuts:
        values = values * shard_levels(stream_key, extent, cuts, -0.22, 0.18)
    return jnp.clip(values, -bound, bound).astype(held_as)


def setup_inputs(seed: int = 0) -> dict:
    splits = jax.random.split(jax.random.key(seed), 15)
    return {
        "tokens": gaussian(splits[0], (M, T_MB, D), 1.0, 6.0, ((1, 64),), jnp.float32),
        "cotangent": gaussian(splits[1], (M, T_MB, D), 1.0, 6.0, ((1, 64),), jnp.float32),
        "seq_lengths": jax.vmap(lambda own: uneven_parts(own, SEQS, T_MB, LONGEST, 2))(jax.random.split(splits[2], M)).reshape((M, SEQS)).astype(jnp.int32),
        "attention_in": gaussian(splits[3], (2, D, 3 * D), D ** -0.5, 0.1875, ((0, 2), (1, 4), (2, 16))),
        "attention_in_bias": gaussian(splits[4], (2, 3 * D), 0.3, 4.0, ((0, 2), (1, 16)), jnp.float32),
        "attention_out": gaussian(splits[5], (2, D, D), (D // 64) ** -0.5, 1.5, ((0, 2), (1, 16), (2, 4))),
        "expand_weight": gaussian(splits[6], (2, D, FF), D ** -0.5, 0.1875, ((0, 2), (1, 4), (2, 16))),
        "expand_bias": gaussian(splits[7], (2, FF), 0.3, 4.0, ((0, 2), (1, 16)), jnp.float32),
        "shrink_weight": gaussian(splits[8], (2, FF, D), FF ** -0.5, 0.09375, ((0, 2), (1, 16), (2, 4))),
        "output_bias": gaussian(splits[9], (2, D), 0.3, 4.0, ((0, 2),), jnp.float32),
        "attend_gain": jnp.clip(1.0 + 0.1 * jax.random.normal(splits[10], (2, D), jnp.float32), 0.5, 1.5),
        "attend_shift": gaussian(splits[11], (2, D), 0.3, 4.0, ((0, 2),), jnp.float32),
        "feed_gain": jnp.clip(1.0 + 0.1 * jax.random.normal(splits[12], (2, D), jnp.float32), 0.5, 1.5),
        "feed_shift": gaussian(splits[13], (2, D), 0.3, 4.0, ((0, 2),), jnp.float32),
    }


@jax.custom_vjp
def low(v):
    return lax.optimization_barrier(v.astype(jnp.bfloat16)).astype(jnp.float32)

@jax.custom_vjp
def low_back(v):
    return v

def low_keep(v):
    return (low(v), None)

def low_pass(kept, grad):
    return (grad,)

def back_keep(v):
    return (v, None)

def back_low(kept, grad):
    return (low(grad),)
low.defvjp(low_keep, low_pass)
low_back.defvjp(back_keep, back_low)
HIGHEST = lax.Precision.HIGHEST
EPSILON = 1e-05

def norm_hat(stream):
    center = stream - lax.optimization_barrier(jnp.mean(stream, axis=-1, keepdims=True))
    spread = lax.optimization_barrier(jnp.mean(center * center, axis=-1, keepdims=True))
    return center * lax.rsqrt(spread + EPSILON)

def layout(lengths, first_token, span):
    lengths = lengths.astype(jnp.int32)
    seq_ends = jnp.cumsum(lengths).astype(jnp.int32)
    token_index = (first_token + jnp.arange(span)).astype(jnp.int32)
    passed = token_index[:, None] >= seq_ends[None, :]
    segment = lax.optimization_barrier(jnp.sum(passed.astype(jnp.int32), axis=1)).astype(jnp.int32)
    position = token_index - lax.optimization_barrier(jnp.sum(jnp.where(passed, lengths[None, :], 0), axis=1)).astype(jnp.int32)
    return (segment, position, token_index)

def turn_tables(position):
    half_turn = ROT // 2
    frequency = 10000.0 ** (-(jnp.arange(half_turn, dtype=jnp.float32) * 2.0) / ROT)
    angles = position.astype(jnp.float32)[:, None] * jnp.concatenate([frequency, frequency])[None, :]
    return (jnp.cos(angles), jnp.sin(angles))

def rotate(values, cosine_table, sine_table):
    half_turn = ROT // 2
    turned_part = values[..., :ROT]
    swapped = jnp.concatenate([-turned_part[..., half_turn:], turned_part[..., :half_turn]], axis=-1)
    return jnp.concatenate([turned_part * cosine_table + swapped * sine_table, values[..., ROT:]], axis=-1)

def layer(stream, params, lengths):
    attention_in, attention_in_bias, attention_out, expand_weight, expand_bias, shrink_weight, output_bias, attend_gain, attend_shift, feed_gain, feed_shift = params
    row_total = stream.shape[0]
    normed = low(norm_hat(stream))
    attend_in = low(attend_gain * normed + attend_shift)
    feed_in = low(feed_gain * normed + feed_shift)
    joint_rows = low_back(jnp.dot(attend_in, attention_in, precision=HIGHEST) + attention_in_bias)
    joint_rows = joint_rows.reshape(row_total, H, 3, HD).transpose(1, 2, 0, 3)
    segment, position, token_index = layout(lengths, 0, row_total)
    cosine_table, sine_table = turn_tables(position)
    queries = low(rotate(joint_rows[:, 0], cosine_table, sine_table))
    key_rows = low(rotate(joint_rows[:, 1], cosine_table, sine_table))
    values = low(joint_rows[:, 2])
    allowed = (segment[:, None] == segment[None, :]) & (token_index[None, :] <= token_index[:, None])
    score_scale = 1.0 / math.sqrt(HD)

    def one_head(pieces):
        head_query, head_keys, head_values = pieces
        scores = low_back(jnp.dot(head_query, head_keys.T, precision=HIGHEST) * score_scale)
        scores = jnp.where(allowed, scores, -jnp.inf)
        probabilities = jax.nn.softmax(scores, axis=-1)
        return low_back(low(jnp.dot(low(probabilities), head_values, precision=HIGHEST)))
    heads_out = lax.map(jax.checkpoint(one_head), (queries, key_rows, values))
    heads_out = heads_out.transpose(1, 0, 2).reshape(row_total, D)
    preact = low_back(jnp.dot(feed_in, expand_weight, precision=HIGHEST) + expand_bias)
    hidden = low(jax.nn.gelu(preact, approximate=False))
    branch = low_back(jnp.dot(heads_out, attention_out, precision=HIGHEST) + jnp.dot(hidden, shrink_weight, precision=HIGHEST) + output_bias)
    return stream + branch

def reference(tokens, cotangent, seq_lengths, attention_in, attention_in_bias, attention_out, expand_weight, expand_bias, shrink_weight, output_bias, attend_gain, attend_shift, feed_gain, feed_shift):
    weight_list = (attention_in, attention_in_bias, attention_out, expand_weight, expand_bias, shrink_weight, output_bias, attend_gain, attend_shift, feed_gain, feed_shift)

    def section_params(which):
        return tuple((weight_array[which].astype(jnp.float32) for weight_array in weight_list))

    def run(stream_all, params):
        return jnp.stack([layer(stream_all[micro_index], params, seq_lengths[micro_index]) for micro_index in range(M)])
    first_out, first_back = jax.vjp(run, tokens.astype(jnp.float32), section_params(0))
    second_out, second_back = jax.vjp(run, first_out, section_params(1))
    middle_grad, second_grads = second_back(cotangent.astype(jnp.float32))
    input_grad, first_grads = first_back(middle_grad)
    stacked = [jnp.stack([first_part, second_part]) for first_part, second_part in zip(first_grads, second_grads)]
    return (jnp.stack([first_out, second_out]), jnp.stack([input_grad, middle_grad]), stacked[0], stacked[1], stacked[2], stacked[3], stacked[4], stacked[5], stacked[6], stacked[7], stacked[8], stacked[9], stacked[10])
```

```python
import functools
import math

import jax
import jax.numpy as jnp
from jax import lax
from jax.experimental import pallas as pl
from jax.experimental.pallas import tpu as pltpu
from jax.sharding import PartitionSpec as P

D = 1024
HD = 64
ROT = 16
EPSILON = 1e-05
BLOCK = 64
GROUP = 1024
WINDOW = 3
TQ = 256
TK = 512
LOW = -1e30

bf16 = jnp.bfloat16
f32 = jnp.float32


def col_pairs(stage, by):
    pairs = []
    for core in range(2):
        along_y = (stage == 1) == (core == 0)
        for z in range(4):
            for y in range(4):
                to = (z * 4 + (y + by) % 4) if along_y else (((z + by) % 4) * 4 + y)
                pairs.append((core * 16 + z * 4 + y, core * 16 + to))
    return pairs


def col_shift(value, stage, by):
    return lax.ppermute(value, ("section", "col"), col_pairs(stage, by))


def row_shift(value, by):
    return lax.ppermute(value, "row", [(i, (i + by) % 4) for i in range(4)])


def swap(value):
    return lax.ppermute(value, "section", [(0, 1), (1, 0)])


def gather_col(rows):
    near = [rows] + [col_shift(rows, 1, k) for k in (1, 2, 3)]
    plane = jnp.concatenate(near, axis=0)
    return [plane] + [col_shift(plane, 2, k) for k in (1, 2, 3)]


def scatter_col(chunks):
    got = [col_shift(chunks[k], 2, -k) for k in (1, 2, 3)]
    plane = chunks[0].astype(f32) + sum(piece.astype(f32) for piece in got)
    parts = plane.astype(bf16).reshape(4, BLOCK, D)
    got = [col_shift(parts[k], 1, -k) for k in (1, 2, 3)]
    return plane.reshape(4, BLOCK, D)[0] + sum(piece.astype(f32) for piece in got)


def contract(left_side, right_side, left_dim, right_dim):
    return lax.dot_general(
        left_side,
        right_side,
        (((left_dim,), (right_dim,)), ((), ())),
        preferred_element_type=f32,
    )


def first_key(token, meta):
    start = jnp.zeros_like(token)
    end = 0
    for index in range(4):
        end = end + meta[index]
        start = jnp.where(token >= end, end, start)
    return start


def tile_mask(meta, row, low_token, key_token):
    query_token = low_token + lax.broadcasted_iota(jnp.int32, (TQ, 1), 0)
    start = first_key(query_token, meta)
    keys = key_token + lax.broadcasted_iota(jnp.int32, (1, TK), 1)
    return (keys >= start) & (keys <= query_token)


def to_order(meta, source, target, groups):
    for block in range(16):
        place = pl.multiple_of(meta[8 + block] * BLOCK, BLOCK)
        for from_group, to_group in groups:
            target[pl.ds(to_group * GROUP + place, BLOCK), :] = source[
                from_group * GROUP + block * BLOCK : from_group * GROUP + (block + 1) * BLOCK, :
            ]


def key_range(meta, row, tile):
    low_token = row * GROUP + tile * TQ
    base = (row - 2) * GROUP
    lowest = (first_key(low_token, meta) - base) // TK
    highest = (2 * GROUP + tile * TQ + TQ - 1) // TK
    return low_token, base, lowest, highest + 1


def attend_kernel(meta, q_ref, k0_ref, k1_ref, k2_ref, out_ref, exact_ref, lse_ref, q_s, kv_s, o_s):
    row = meta[4]
    to_order(meta, q_ref, q_s, [(0, 0)])
    for group, ref in ((0, k2_ref), (1, k1_ref), (2, k0_ref)):
        to_order(meta, ref, kv_s, [(0, group)])
    upper = lax.broadcasted_iota(jnp.int32, (TQ, 2 * HD), 1) >= HD

    def per_tile(tile, carry):
        rows = pl.ds(pl.multiple_of(tile * TQ, TQ), TQ)
        query = q_s[rows, :]
        low_token, base, lowest, highest = key_range(meta, row, tile)

        def step(index, state):
            top, total, acc = state
            kv = kv_s[pl.ds(pl.multiple_of(index * TK, TK), TK), :]
            scores = contract(query, kv, 1, 1)
            mask = tile_mask(meta, row, low_token, base + index * TK)
            scores = jnp.where(mask, scores, LOW)
            new_top = jnp.maximum(top, jnp.max(scores, axis=1, keepdims=True))
            weight = jnp.exp(scores - new_top)
            shrink = jnp.exp(top - new_top)
            total = total * shrink + jnp.sum(weight, axis=1, keepdims=True)
            acc = acc * shrink + contract(weight.astype(bf16), kv, 1, 0)
            return new_top, total, acc

        top, total, acc = lax.fori_loop(
            lowest,
            highest,
            step,
            (
                jnp.full((TQ, 1), LOW, f32),
                jnp.zeros((TQ, 1), f32),
                jnp.zeros((TQ, 2 * HD), f32),
            ),
        )
        exact = jnp.where(upper, acc / total, 0.0)
        exact_ref[rows, :] = exact
        o_s[rows, :] = exact.astype(bf16)
        lse_ref[rows, :] = top + jnp.log(total)
        return carry

    lax.fori_loop(0, GROUP // TQ, per_tile, 0)
    for block in range(16):
        place = pl.multiple_of(meta[8 + block] * BLOCK, BLOCK)
        out_ref[block * BLOCK : (block + 1) * BLOCK, :] = o_s[pl.ds(place, BLOCK), :]


def attend_back_kernel(
    meta, q_ref, k0_ref, k1_ref, k2_ref, g_ref, exact_ref, lse_ref,
    dq_ref, d0_ref, d1_ref, d2_ref, q_s, kv_s, g_s, dq_s, dkv_s,
):
    row = meta[4]
    to_order(meta, q_ref, q_s, [(0, 0)])
    to_order(meta, g_ref, g_s, [(0, 0)])
    for group, ref in ((0, k2_ref), (1, k1_ref), (2, k0_ref)):
        to_order(meta, ref, kv_s, [(0, group)])
    dkv_s[...] = jnp.zeros_like(dkv_s)

    def per_tile(tile, carry):
        rows = pl.ds(pl.multiple_of(tile * TQ, TQ), TQ)
        query = q_s[rows, :]
        grad = g_s[rows, :]
        lse = lse_ref[rows, :]
        delta = jnp.sum(grad.astype(f32) * exact_ref[rows, :], axis=1, keepdims=True)
        low_token, base, lowest, highest = key_range(meta, row, tile)

        def step(index, dq):
            keys = pl.ds(pl.multiple_of(index * TK, TK), TK)
            kv = kv_s[keys, :]
            scores = contract(query, kv, 1, 1)
            mask = tile_mask(meta, row, low_token, base + index * TK)
            probs = jnp.exp(jnp.where(mask, scores, LOW) - lse)
            grad_probs = contract(grad, kv, 1, 1)
            grad_scores = (probs * (grad_probs - delta)).astype(bf16)
            dkv_s[keys, :] += contract(grad_scores, query, 0, 0) + contract(
                probs.astype(bf16), grad, 0, 0
            )
            return dq + contract(grad_scores, kv, 1, 0)

        dq_s[rows, :] = lax.fori_loop(lowest, highest, step, jnp.zeros((TQ, 2 * HD), f32))
        return carry

    lax.fori_loop(0, GROUP // TQ, per_tile, 0)
    lower = lax.broadcasted_iota(jnp.int32, (BLOCK, 2 * HD), 1) < HD
    for block in range(16):
        place = pl.multiple_of(meta[8 + block] * BLOCK, BLOCK)
        here = slice(block * BLOCK, (block + 1) * BLOCK)
        dq_ref[here, :] = jnp.where(lower, dq_s[pl.ds(place, BLOCK), :] * (1.0 / math.sqrt(HD)), 0.0)
        for group, ref in ((0, d2_ref), (1, d1_ref), (2, d0_ref)):
            ref[here, :] = dkv_s[pl.ds(group * GROUP + place, BLOCK), :].astype(bf16)


VMEM = pl.BlockSpec(memory_space=pltpu.VMEM)
SMEM = pl.BlockSpec(memory_space=pltpu.SMEM)


def attend(meta, q, kvs):
    wide = (GROUP, 2 * HD)
    return pl.pallas_call(
        attend_kernel,
        out_shape=(
            jax.ShapeDtypeStruct(wide, bf16),
            jax.ShapeDtypeStruct(wide, f32),
            jax.ShapeDtypeStruct((GROUP, 1), f32),
        ),
        in_specs=[SMEM] + [VMEM] * 4,
        out_specs=(VMEM,) * 3,
        scratch_shapes=[
            pltpu.VMEM(wide, bf16),
            pltpu.VMEM((WINDOW * GROUP, 2 * HD), bf16),
            pltpu.VMEM(wide, bf16),
        ],
        compiler_params=pltpu.CompilerParams(vmem_limit_bytes=24 * 2**20),
        cost_estimate=pl.CostEstimate(
            flops=2_000_000_000, bytes_accessed=3_000_000, transcendentals=2_000_000
        ),
        name="attend",
    )(meta, q, *kvs)


def attend_back(meta, q, kvs, grad, exact, lse):
    wide = (GROUP, 2 * HD)
    return pl.pallas_call(
        attend_back_kernel,
        out_shape=(jax.ShapeDtypeStruct(wide, f32),) + (jax.ShapeDtypeStruct(wide, bf16),) * 3,
        in_specs=[SMEM] + [VMEM] * 7,
        out_specs=(VMEM,) * 4,
        scratch_shapes=[
            pltpu.VMEM(wide, bf16),
            pltpu.VMEM((WINDOW * GROUP, 2 * HD), bf16),
            pltpu.VMEM(wide, bf16),
            pltpu.VMEM(wide, f32),
            pltpu.VMEM((WINDOW * GROUP, 2 * HD), f32),
        ],
        compiler_params=pltpu.CompilerParams(vmem_limit_bytes=24 * 2**20),
        cost_estimate=pl.CostEstimate(
            flops=5_000_000_000, bytes_accessed=5_000_000, transcendentals=2_000_000
        ),
        name="attend_back",
    )(meta, q, *kvs, grad, exact, lse)


def norm_parts(stream):
    center = stream - jnp.mean(stream, axis=-1, keepdims=True)
    spread = jnp.mean(center * center, axis=-1, keepdims=True)
    scale = lax.rsqrt(spread + EPSILON)
    return center * scale, scale


def turn_tables(position):
    half_turn = ROT // 2
    frequency = 10000.0 ** (-(jnp.arange(half_turn, dtype=f32) * 2.0) / ROT)
    angles = position.astype(f32)[:, None] * jnp.concatenate([frequency, frequency])[None, :]
    sign = jnp.where(jnp.arange(ROT) < half_turn, -1.0, 1.0)
    rest = 2 * HD - ROT
    rows = position.shape[0]
    cosine = jnp.concatenate([jnp.cos(angles), jnp.ones((rows, rest), f32)], axis=1)
    sine = jnp.concatenate([jnp.sin(angles) * sign, jnp.zeros((rows, rest), f32)], axis=1)
    return cosine, sine


def turn(value, cosine, sine):
    half_turn = ROT // 2
    swapped = jnp.concatenate(
        [value[:, half_turn:ROT], value[:, :half_turn], value[:, ROT:]], axis=1
    )
    return value * cosine + swapped * sine


def on_device(
    tokens,
    cotangent,
    seq_lengths,
    attention_in,
    attention_in_bias,
    attention_out,
    expand_weight,
    expand_bias,
    shrink_weight,
    output_bias,
    attend_gain,
    attend_shift,
    feed_gain,
    feed_shift,
):
    row = lax.axis_index("row")
    col = lax.axis_index("col")
    section = lax.axis_index("section")
    first = section == 0
    pick = lambda a, b: jnp.where(first, a, b)

    own = attention_in[0]
    shard = jnp.stack(
        [
            jnp.concatenate([own[:, :HD], attention_out[0].T, own[:, HD:]], axis=1),
            expand_weight[0],
            shrink_weight[0].T,
        ]
    )
    mine = jnp.zeros((3, D, 256), bf16)
    for k in range(4):
        piece = shard if k == 0 else row_shift(shard, -k)
        mine = lax.dynamic_update_slice(mine, piece, (0, ((row + k) % 4) * 256, 0))
    theirs = swap(mine)
    whole = (pick(mine, theirs), pick(theirs, mine))

    vectors = jnp.concatenate(
        [
            attend_gain,
            attend_shift,
            feed_gain,
            feed_shift,
            output_bias,
            jnp.concatenate(
                [
                    attention_in_bias[:, :HD],
                    jnp.zeros((1, HD), f32),
                    attention_in_bias[:, HD:],
                    expand_bias,
                    jnp.zeros((1, 512), f32),
                ],
                axis=1,
            ),
        ],
        axis=0,
    )
    their_vectors = swap(vectors)
    vector_sets = (pick(vectors, their_vectors), pick(their_vectors, vectors))

    lane = jnp.arange(256)
    qkv_lanes = ((lane < HD) | (lane >= 2 * HD))[None, :]
    out_lanes = (lane[: 2 * HD] >= HD)[None, :]

    lengths = pick(seq_lengths[0], seq_lengths[1])
    y, z = col % 4, col // 4
    near, far = pick(y, z), pick(z, y)
    block = jnp.arange(16)
    near_at, far_at = (near - block % 4) % 4, (far - block // 4) % 4
    places = pick(far_at * 4 + near_at, near_at * 4 + far_at)
    token = row * GROUP + (places[:, None] * BLOCK + jnp.arange(BLOCK)[None, :]).reshape(GROUP)
    position = token - first_key(token, lengths)
    cosine, sine = turn_tables(position)
    meta = jnp.concatenate(
        [lengths, row[None], jnp.zeros((3,), jnp.int32), places]
    ).astype(jnp.int32)

    piece = lambda value, j: value[j * 256 : (j + 1) * 256]

    def weights_of(layer):
        pack = whole[layer]
        qkv = jnp.where(qkv_lanes, pack[0], jnp.zeros((), bf16))
        out = jnp.where(out_lanes, pack[0][:, : 2 * HD], jnp.zeros((), bf16))
        return qkv, pack[1], out, pack[2]

    def forward(layer, stream):
        qkv, expand, out, shrink = weights_of(layer)
        vec = vector_sets[layer]
        unit, scale = norm_parts(stream)
        normed = gather_col(unit.astype(bf16))
        attend_in, feed_in, q, kv, hidden, slope = [], [], [], [], [], []
        for j in range(4):
            attend_in.append((vec[0] * normed[j] + vec[1]).astype(bf16))
            joint = contract(attend_in[j], qkv, 1, 0) + vec[5, :256]
            c, s = piece(cosine, j), piece(sine, j)
            q.append((turn(joint[:, : 2 * HD], c, s)).astype(bf16) * bf16(1.0 / math.sqrt(HD)))
            kv.append(turn(joint[:, 2 * HD :], c, s).astype(bf16))
        q, kv = jnp.concatenate(q), jnp.concatenate(kv)
        kvs = (kv, row_shift(kv, 1), row_shift(kv, 2))
        for j in range(4):
            feed_in.append((vec[2] * normed[j] + vec[3]).astype(bf16))
            pre = contract(feed_in[j], expand, 1, 0) + vec[5, 256:512]
            cdf = 0.5 * (1.0 + lax.erf(pre * math.sqrt(0.5)))
            hidden.append((pre * cdf).astype(bf16))
            slope.append(cdf + pre * jnp.exp(-0.5 * pre * pre) * (1.0 / math.sqrt(2 * math.pi)))
        heads, exact, lse = attend(meta, q, kvs)
        partial = [
            (contract(piece(heads, j), out, 1, 1) + contract(hidden[j], shrink, 1, 1)).astype(bf16)
            for j in range(4)
        ]
        result = stream + (scatter_col(partial) + vec[4])
        saved = (unit, scale, normed, attend_in, feed_in, q, kvs, heads, exact, lse, hidden, slope)
        return result, saved

    def backward(layer, grad_out, saved):
        unit, scale, normed, attend_in, feed_in, q, kvs, heads, exact, lse, hidden, slope = saved
        qkv, expand, out, shrink = weights_of(layer)
        vec = vector_sets[layer]
        branch = grad_out.astype(bf16)
        grads = gather_col(branch)
        grad_heads = jnp.concatenate([contract(grads[j], out, 1, 0).astype(bf16) for j in range(4)])
        dq, d0, d1, d2 = attend_back(meta, q, kvs, grad_heads, exact, lse)
        got1, got2 = row_shift(d1, -1), row_shift(d2, -2)
        grad_pre = [(contract(grads[j], shrink, 1, 0) * slope[j]).astype(bf16) for j in range(4)]
        grad_feed = [contract(grad_pre[j], expand, 1, 1) for j in range(4)]
        grads, grad_pre_all = jnp.concatenate(grads), jnp.concatenate(grad_pre)
        d_out = contract(grads, heads, 0, 0)
        d_shrink = contract(grads, jnp.concatenate(hidden), 0, 0)
        d_expand = contract(jnp.concatenate(feed_in), grad_pre_all, 0, 0)
        dkv = d0.astype(f32) + got1.astype(f32) + got2.astype(f32)
        grad_joint = jnp.concatenate(
            [turn(dq, cosine, -sine), turn(dkv, cosine, -sine)], axis=1
        ).astype(bf16)
        grad_attend = [contract(piece(grad_joint, j), qkv, 1, 1) for j in range(4)]
        summed = scatter_col(
            [(vec[0] * grad_attend[j] + vec[2] * grad_feed[j]).astype(bf16) for j in range(4)]
        )
        d_in = contract(jnp.concatenate(attend_in), grad_joint, 0, 0)
        over = lambda make: sum(jnp.sum(make(j), axis=0) for j in range(4))
        smalls = jnp.stack(
            [
                over(lambda j: normed[j].astype(f32) * grad_attend[j]),
                over(lambda j: grad_attend[j]),
                over(lambda j: normed[j].astype(f32) * grad_feed[j]),
                over(lambda j: grad_feed[j]),
                jnp.sum(branch.astype(f32), axis=0),
                jnp.concatenate(
                    [
                        jnp.sum(grad_joint.astype(f32), axis=0),
                        jnp.sum(grad_pre_all.astype(f32), axis=0),
                        jnp.zeros((512,), f32),
                    ]
                ),
            ]
        )
        inner = (
            summed
            - jnp.mean(summed, axis=-1, keepdims=True)
            - unit * jnp.mean(summed * unit, axis=-1, keepdims=True)
        )
        matrices = jnp.stack(
            [d_in + jnp.pad(d_out, ((0, 0), (0, 2 * HD))), d_expand, d_shrink]
        ).astype(bf16)
        return grad_out + inner * scale, matrices, smalls

    stream = pick(tokens[0], tokens[1])
    middle, saved0 = forward(0, stream)
    last, saved1 = forward(1, middle)
    middle_grad, matrices1, smalls1 = backward(1, pick(cotangent[0], cotangent[1]), saved1)
    input_grad, matrices0, smalls0 = backward(0, middle_grad, saved0)

    def settle(of_first, of_second):
        return pick(of_first, of_second), swap(pick(of_second, of_first))

    kept, other = settle(matrices0, matrices1)
    total = kept.astype(f32) + other.astype(f32)
    part = lambda k: lax.dynamic_slice(total, (0, ((row + k) % 4) * 256, 0), (3, 256, 256))
    matrices = part(0) + sum(
        row_shift(part(k).astype(bf16), k).astype(f32) for k in (1, 2, 3)
    )

    kept, other = settle(smalls0, smalls1)
    sums = kept + other
    sums = sums + sum(row_shift(sums, k) for k in (1, 2, 3))
    biases, sums = sums[5], sums[:5]
    for stage in (1, 2):
        sums = sums + sum(col_shift(sums, stage, k) for k in (1, 2, 3))

    def by_batch(of_first, of_second):
        kept, other = settle(of_first, of_second)
        return pick(jnp.stack([kept, other]), jnp.stack([other, kept]))[None]

    packed = matrices[0]
    return (
        by_batch(middle, last),
        by_batch(input_grad, middle_grad),
        jnp.concatenate([packed[:, :HD], packed[:, 2 * HD :]], axis=1)[None],
        jnp.concatenate([biases[:HD], biases[2 * HD : 256]])[None],
        packed[:, HD : 2 * HD].T[None],
        matrices[1][None],
        biases[256:512][None],
        matrices[2].T[None],
        sums[4][None],
        sums[0][None],
        sums[1][None],
        sums[2][None],
        sums[3][None],
    )


def solution(mesh):
    return jax.shard_map(
        on_device,
        mesh=mesh,
        in_specs=(
            P(None, ("row", "col"), None),
            P(None, ("row", "col"), None),
            P(),
            P("section", "row", "col"),
            P("section", "col"),
            P("section", "col", "row"),
            P("section", "row", "col"),
            P("section", "col"),
            P("section", "col", "row"),
            P("section", None),
            P("section", None),
            P("section", None),
            P("section", None),
            P("section", None),
        ),
        out_specs=(
            P("section", None, ("row", "col"), None),
            P("section", None, ("row", "col"), None),
            P("section", "row", "col"),
            P("section", "col"),
            P("section", "col", "row"),
            P("section", "row", "col"),
            P("section", "col"),
            P("section", "col", "row"),
            P("section", None),
            P("section", None),
            P("section", None),
            P("section", None),
            P("section", None),
        ),
        check_vma=False,
    )
```

```python
import functools
import math

import jax
import jax.numpy as jnp
from jax import lax
from jax.experimental import pallas as pl
from jax.experimental.pallas import tpu as pltpu
from jax.sharding import PartitionSpec as P

D = 1024
HD = 64
ROT = 16
EPSILON = 1e-05
BLOCK = 64
GROUP = 1024
WINDOW = 3
TQ = 256
TK = 512
LOW = -1e30

bf16 = jnp.bfloat16
f32 = jnp.float32


def col_pairs(stage, by):
    pairs = []
    for core in range(2):
        along_y = (stage == 1) == (core == 0)
        for z in range(4):
            for y in range(4):
                to = (z * 4 + (y + by) % 4) if along_y else (((z + by) % 4) * 4 + y)
                pairs.append((core * 16 + z * 4 + y, core * 16 + to))
    return pairs


def col_shift(value, stage, by):
    return lax.ppermute(value, ("section", "col"), col_pairs(stage, by))


def row_shift(value, by):
    return lax.ppermute(value, "row", [(i, (i + by) % 4) for i in range(4)])


def swap(value):
    return lax.ppermute(value, "section", [(0, 1), (1, 0)])


def gather_near(rows):
    return jnp.concatenate([rows] + [col_shift(rows, 1, k) for k in (1, 2, 3)], axis=0)


def gather_far(plane):
    return [plane] + [col_shift(plane, 2, k) for k in (1, 2, 3)]


def gather_col(rows):
    return gather_far(gather_near(rows))


def scatter_far(chunks):
    return far_sum(chunks, far_pieces(chunks))


def far_pieces(chunks):
    return [col_shift(chunks[k], 2, -k) for k in (1, 2, 3)]


def far_sum(chunks, got):
    return chunks[0].astype(f32) + sum(piece.astype(f32) for piece in got)


def scatter_near(plane):
    plane = plane.reshape(4, BLOCK, D)
    got = [col_shift(plane[k].astype(bf16), 1, -k) for k in (1, 2, 3)]
    return plane[0] + sum(piece.astype(f32) for piece in got)


def contract(left_side, right_side, left_dim, right_dim):
    return lax.dot_general(
        left_side,
        right_side,
        (((left_dim,), (right_dim,)), ((), ())),
        preferred_element_type=f32,
    )


def first_key(token, meta):
    start = jnp.zeros_like(token)
    end = 0
    for index in range(4):
        end = end + meta[index]
        start = jnp.where(token >= end, end, start)
    return start


def tile_mask(meta, row, low_token, key_token):
    query_token = low_token + lax.broadcasted_iota(jnp.int32, (TQ, 1), 0)
    start = first_key(query_token, meta)
    keys = key_token + lax.broadcasted_iota(jnp.int32, (1, TK), 1)
    return (keys >= start) & (keys <= query_token)


def to_order(meta, source, target, groups):
    for block in range(16):
        place = pl.multiple_of(meta[8 + block] * BLOCK, BLOCK)
        for from_group, to_group in groups:
            target[pl.ds(to_group * GROUP + place, BLOCK), :] = source[
                from_group * GROUP + block * BLOCK : from_group * GROUP + (block + 1) * BLOCK, :
            ]


def key_range(meta, row, tile):
    low_token = row * GROUP + tile * TQ
    base = (row - 2) * GROUP
    lowest = (first_key(low_token, meta) - base) // TK
    highest = (2 * GROUP + tile * TQ + TQ - 1) // TK
    return low_token, base, lowest, highest + 1


def attend_kernel(meta, q_ref, k0_ref, k1_ref, k2_ref, out_ref, exact_ref, lse_ref, q_s, kv_s, o_s):
    row = meta[4]
    to_order(meta, q_ref, q_s, [(0, 0)])
    for group, ref in ((0, k2_ref), (1, k1_ref), (2, k0_ref)):
        to_order(meta, ref, kv_s, [(0, group)])
    upper = lax.broadcasted_iota(jnp.int32, (TQ, 2 * HD), 1) >= HD

    def per_tile(tile, carry):
        rows = pl.ds(pl.multiple_of(tile * TQ, TQ), TQ)
        query = q_s[rows, :]
        low_token, base, lowest, highest = key_range(meta, row, tile)

        def step(index, state):
            top, total, acc = state
            kv = kv_s[pl.ds(pl.multiple_of(index * TK, TK), TK), :]
            scores = contract(query, kv, 1, 1)
            mask = tile_mask(meta, row, low_token, base + index * TK)
            scores = jnp.where(mask, scores, LOW)
            new_top = jnp.maximum(top, jnp.max(scores, axis=1, keepdims=True))
            weight = jnp.exp(scores - new_top)
            shrink = jnp.exp(top - new_top)
            total = total * shrink + jnp.sum(weight, axis=1, keepdims=True)
            acc = acc * shrink + contract(weight.astype(bf16), kv, 1, 0)
            return new_top, total, acc

        top, total, acc = lax.fori_loop(
            lowest,
            highest,
            step,
            (
                jnp.full((TQ, 1), LOW, f32),
                jnp.zeros((TQ, 1), f32),
                jnp.zeros((TQ, 2 * HD), f32),
            ),
        )
        exact = jnp.where(upper, acc / total, 0.0)
        exact_ref[rows, :] = exact
        o_s[rows, :] = exact.astype(bf16)
        lse_ref[rows, :] = top + jnp.log(total)
        return carry

    lax.fori_loop(0, GROUP // TQ, per_tile, 0)
    for block in range(16):
        place = pl.multiple_of(meta[8 + block] * BLOCK, BLOCK)
        out_ref[block * BLOCK : (block + 1) * BLOCK, :] = o_s[pl.ds(place, BLOCK), :]


def attend_back_kernel(
    meta, q_ref, k0_ref, k1_ref, k2_ref, g_ref, exact_ref, lse_ref,
    dq_ref, d0_ref, d1_ref, d2_ref, q_s, kv_s, g_s, dq_s, dkv_s,
):
    row = meta[4]
    to_order(meta, q_ref, q_s, [(0, 0)])
    to_order(meta, g_ref, g_s, [(0, 0)])
    for group, ref in ((0, k2_ref), (1, k1_ref), (2, k0_ref)):
        to_order(meta, ref, kv_s, [(0, group)])
    dkv_s[...] = jnp.zeros_like(dkv_s)

    def per_tile(tile, carry):
        rows = pl.ds(pl.multiple_of(tile * TQ, TQ), TQ)
        query = q_s[rows, :]
        grad = g_s[rows, :]
        lse = lse_ref[rows, :]
        delta = jnp.sum(grad.astype(f32) * exact_ref[rows, :], axis=1, keepdims=True)
        low_token, base, lowest, highest = key_range(meta, row, tile)

        def step(index, dq):
            keys = pl.ds(pl.multiple_of(index * TK, TK), TK)
            kv = kv_s[keys, :]
            scores = contract(query, kv, 1, 1)
            mask = tile_mask(meta, row, low_token, base + index * TK)
            probs = jnp.exp(jnp.where(mask, scores, LOW) - lse)
            grad_probs = contract(grad, kv, 1, 1)
            grad_scores = (probs * (grad_probs - delta)).astype(bf16)
            dkv_s[keys, :] += contract(grad_scores, query, 0, 0) + contract(
                probs.astype(bf16), grad, 0, 0
            )
            return dq + contract(grad_scores, kv, 1, 0)

        dq_s[rows, :] = lax.fori_loop(lowest, highest, step, jnp.zeros((TQ, 2 * HD), f32))
        return carry

    lax.fori_loop(0, GROUP // TQ, per_tile, 0)
    lower = lax.broadcasted_iota(jnp.int32, (BLOCK, 2 * HD), 1) < HD
    for block in range(16):
        place = pl.multiple_of(meta[8 + block] * BLOCK, BLOCK)
        here = slice(block * BLOCK, (block + 1) * BLOCK)
        dq_ref[here, :] = jnp.where(lower, dq_s[pl.ds(place, BLOCK), :] * (1.0 / math.sqrt(HD)), 0.0)
        for group, ref in ((0, d2_ref), (1, d1_ref), (2, d0_ref)):
            ref[here, :] = dkv_s[pl.ds(group * GROUP + place, BLOCK), :].astype(bf16)


VMEM = pl.BlockSpec(memory_space=pltpu.VMEM)
SMEM = pl.BlockSpec(memory_space=pltpu.SMEM)


def attend(meta, q, kvs):
    wide = (GROUP, 2 * HD)
    return pl.pallas_call(
        attend_kernel,
        out_shape=(
            jax.ShapeDtypeStruct(wide, bf16),
            jax.ShapeDtypeStruct(wide, f32),
            jax.ShapeDtypeStruct((GROUP, 1), f32),
        ),
        in_specs=[SMEM] + [VMEM] * 4,
        out_specs=(VMEM,) * 3,
        scratch_shapes=[
            pltpu.VMEM(wide, bf16),
            pltpu.VMEM((WINDOW * GROUP, 2 * HD), bf16),
            pltpu.VMEM(wide, bf16),
        ],
        compiler_params=pltpu.CompilerParams(vmem_limit_bytes=24 * 2**20),
        cost_estimate=pl.CostEstimate(
            flops=2_000_000_000, bytes_accessed=3_000_000, transcendentals=2_000_000
        ),
        name="attend",
    )(meta, q, *kvs)


def attend_back(meta, q, kvs, grad, exact, lse):
    wide = (GROUP, 2 * HD)
    return pl.pallas_call(
        attend_back_kernel,
        out_shape=(jax.ShapeDtypeStruct(wide, f32),) + (jax.ShapeDtypeStruct(wide, bf16),) * 3,
        in_specs=[SMEM] + [VMEM] * 7,
        out_specs=(VMEM,) * 4,
        scratch_shapes=[
            pltpu.VMEM(wide, bf16),
            pltpu.VMEM((WINDOW * GROUP, 2 * HD), bf16),
            pltpu.VMEM(wide, bf16),
            pltpu.VMEM(wide, f32),
            pltpu.VMEM((WINDOW * GROUP, 2 * HD), f32),
        ],
        compiler_params=pltpu.CompilerParams(vmem_limit_bytes=24 * 2**20),
        cost_estimate=pl.CostEstimate(
            flops=5_000_000_000, bytes_accessed=5_000_000, transcendentals=2_000_000
        ),
        name="attend_back",
    )(meta, q, *kvs, grad, exact, lse)


def after(value, *others):
    return lax.optimization_barrier((value,) + others)[0]


def turn_lanes(value, cosine, sine):
    lane = lax.broadcasted_iota(jnp.int32, value.shape, 1)
    swapped = jnp.where(
        lane < ROT // 2,
        pltpu.roll(value, 2 * HD - ROT // 2, 1),
        pltpu.roll(value, ROT // 2, 1),
    )
    return value * cosine + swapped * sine


def project_kernel(
    n0, n1, n2, n3, weight, bias, gain, shift, cosine, sine, attend_out, q_out, kv_out
):
    lower = lax.broadcasted_iota(jnp.int32, (256, 2 * HD), 1) < HD
    for j, normed in enumerate((n0, n1, n2, n3)):
        rows = slice(j * 256, (j + 1) * 256)
        attend_in = (gain[...] * normed[...].astype(f32) + shift[...]).astype(bf16)
        attend_out[rows, :] = attend_in
        joint = contract(attend_in, weight[...], 1, 0) + bias[...]
        c, s = cosine[rows, :], sine[rows, :]
        q = turn_lanes(joint[:, : 2 * HD], c, s).astype(bf16).astype(f32)
        q_out[rows, :] = jnp.where(lower, q * (1.0 / math.sqrt(HD)), 0.0).astype(bf16)
        kv_out[rows, :] = turn_lanes(joint[:, 2 * HD :], c, s).astype(bf16)


def project(normed, weight, bias, gain, shift, cosine, sine):
    wide = jax.ShapeDtypeStruct((GROUP, 2 * HD), bf16)
    return pl.pallas_call(
        project_kernel,
        out_shape=(jax.ShapeDtypeStruct((GROUP, D), bf16), wide, wide),
        in_specs=[VMEM] * 10,
        out_specs=(VMEM,) * 3,
        compiler_params=pltpu.CompilerParams(vmem_limit_bytes=24 * 2**20),
        cost_estimate=pl.CostEstimate(
            flops=2 * GROUP * D * 256, bytes_accessed=6 * 2**20, transcendentals=0
        ),
        name="project",
    )(*normed, weight, bias, gain, shift, cosine, sine)


def back_kernel(gj, gp, mixed, expand, gain_a, gain_f, normed, out_ref, sums_ref):
    grad_attend = contract(gj[...], mixed[...], 1, 1)
    grad_feed = contract(gp[...], expand[...], 1, 1)
    out_ref[...] = (gain_a[...] * grad_attend + gain_f[...] * grad_feed).astype(bf16)
    wide = normed[...].astype(f32)
    sums_ref[0:1, :] = jnp.sum(wide * grad_attend, axis=0, keepdims=True)
    sums_ref[1:2, :] = jnp.sum(grad_attend, axis=0, keepdims=True)
    sums_ref[2:3, :] = jnp.sum(wide * grad_feed, axis=0, keepdims=True)
    sums_ref[3:4, :] = jnp.sum(grad_feed, axis=0, keepdims=True)


def back_project(gj, gp, mixed, expand, gain_a, gain_f, normed):
    return pl.pallas_call(
        back_kernel,
        out_shape=(
            jax.ShapeDtypeStruct((256, D), bf16),
            jax.ShapeDtypeStruct((4, D), f32),
        ),
        in_specs=[VMEM] * 7,
        out_specs=(VMEM,) * 2,
        compiler_params=pltpu.CompilerParams(vmem_limit_bytes=16 * 2**20),
        cost_estimate=pl.CostEstimate(
            flops=4 * 256 * D * 256, bytes_accessed=3 * 2**20, transcendentals=0
        ),
        name="back_project",
    )(gj, gp, mixed, expand, gain_a, gain_f, normed)


def pair_sum(value, axis, step, count):
    for flip in (1, 3):
        pairs = [(i, i + (((i // step) % 4 ^ flip) - (i // step) % 4) * step) for i in range(count)]
        value = value + lax.ppermute(value, axis, pairs)
    return value


def norm_parts(stream):
    center = stream - jnp.mean(stream, axis=-1, keepdims=True)
    spread = jnp.mean(center * center, axis=-1, keepdims=True)
    scale = lax.rsqrt(spread + EPSILON)
    return center * scale, scale


def turn_tables(position):
    half_turn = ROT // 2
    frequency = 10000.0 ** (-(jnp.arange(half_turn, dtype=f32) * 2.0) / ROT)
    angles = position.astype(f32)[:, None] * jnp.concatenate([frequency, frequency])[None, :]
    sign = jnp.where(jnp.arange(ROT) < half_turn, -1.0, 1.0)
    rest = 2 * HD - ROT
    rows = position.shape[0]
    cosine = jnp.concatenate([jnp.cos(angles), jnp.ones((rows, rest), f32)], axis=1)
    sine = jnp.concatenate([jnp.sin(angles) * sign, jnp.zeros((rows, rest), f32)], axis=1)
    return cosine, sine


def turn(value, cosine, sine):
    half_turn = ROT // 2
    swapped = jnp.concatenate(
        [value[:, half_turn:ROT], value[:, :half_turn], value[:, ROT:]], axis=1
    )
    return value * cosine + swapped * sine


def on_device(
    tokens,
    cotangent,
    seq_lengths,
    attention_in,
    attention_in_bias,
    attention_out,
    expand_weight,
    expand_bias,
    shrink_weight,
    output_bias,
    attend_gain,
    attend_shift,
    feed_gain,
    feed_shift,
):
    row = lax.axis_index("row")
    col = lax.axis_index("col")
    section = lax.axis_index("section")
    first = section == 0
    pick = lambda a, b: jnp.where(first, a, b)

    stream0 = pick(tokens[0], tokens[1])
    unit0, scale0 = norm_parts(stream0)
    plane0 = gather_near(unit0.astype(bf16))
    chunks0 = gather_far(plane0)

    vectors = jnp.concatenate(
        [
            attend_gain,
            attend_shift,
            feed_gain,
            feed_shift,
            output_bias,
            jnp.concatenate(
                [
                    attention_in_bias[:, :HD],
                    jnp.zeros((1, HD), f32),
                    attention_in_bias[:, HD:],
                    expand_bias,
                    jnp.zeros((1, 512), f32),
                ],
                axis=1,
            ),
        ],
        axis=0,
    )
    their_vectors = swap(vectors)
    vector_sets = (pick(vectors, their_vectors), pick(their_vectors, vectors))

    lengths = pick(seq_lengths[0], seq_lengths[1])
    y, z = col % 4, col // 4
    near, far = pick(y, z), pick(z, y)
    block = jnp.arange(16)
    near_at, far_at = (near - block % 4) % 4, (far - block // 4) % 4
    places = pick(far_at * 4 + near_at, near_at * 4 + far_at)
    token = row * GROUP + (places[:, None] * BLOCK + jnp.arange(BLOCK)[None, :]).reshape(GROUP)
    position = token - first_key(token, after(lengths, plane0))
    cosine, sine = turn_tables(position)
    meta = jnp.concatenate(
        [lengths, row[None], jnp.zeros((3,), jnp.int32), places]
    ).astype(jnp.int32)

    piece = lambda value, j: value[j * 256 : (j + 1) * 256]

    own = attention_in[0]
    mixed = jnp.concatenate([own[:, :HD], attention_out[0].T, own[:, HD:]], axis=1)
    theirs = swap(mixed)
    mixed = after(jnp.stack([pick(mixed, theirs), pick(theirs, mixed)]), plane0)
    near = [mixed] + [row_shift(mixed, -k) for k in (1, 2, 3)]
    near = after(near, chunks0, cosine, sine)
    near = jnp.concatenate(near + near[:3], axis=1)
    near = lax.dynamic_slice(near, (0, ((4 - row) % 4) * 256, 0), (2, D, 256))
    whole_mixed = (near[0], near[1])
    mine = lax.all_gather(
        jnp.stack([expand_weight[0], shrink_weight[0].T]), "row", axis=1, tiled=True
    )
    theirs = swap(mine)
    whole_feed = (pick(mine, theirs), pick(theirs, mine))

    held = {}
    upper = (jnp.arange(2 * HD) >= HD)[None, :]

    def branch_of(layer, heads, hidden):
        out, shrink = whole_mixed[layer][:, : 2 * HD], whole_feed[layer][1]
        return [
            (contract(piece(heads, j), out, 1, 1) + contract(hidden[j], shrink, 1, 1)).astype(bf16)
            for j in range(4)
        ]

    def grads_of(layer, grads):
        out = whole_mixed[layer][:, : 2 * HD]
        return jnp.concatenate(
            [jnp.where(upper, contract(grads[j], out, 1, 0), 0.0).astype(bf16) for j in range(4)]
        )

    def forward(layer, stream):
        vec = vector_sets[layer]
        if layer == 0:
            unit, scale, normed = unit0, scale0, chunks0
        else:
            unit, scale = norm_parts(stream)
            normed = gather_col(unit.astype(bf16))
        attend_in, q, kv = project(
            normed, whole_mixed[layer], vec[5:6, :256], vec[0:1], vec[1:2], cosine, sine
        )
        kvs = (kv, row_shift(kv, 1), row_shift(kv, 2))
        if layer == 0:
            branch = pick(cotangent[0], cotangent[1]).astype(bf16)
            held["grads"] = gather_col(after(branch, q))
        feed_in, hidden, slope = [], [], []
        for j in range(4):
            feed_in.append((vec[2] * normed[j] + vec[3]).astype(bf16))
            pre = contract(feed_in[j], whole_feed[layer][0], 1, 0) + vec[5, 256:512]
            cdf = 0.5 * (1.0 + lax.erf(pre * math.sqrt(0.5)))
            hidden.append((pre * cdf).astype(bf16))
            slope.append(cdf + pre * jnp.exp(-0.5 * pre * pre) * (1.0 / math.sqrt(2 * math.pi)))
        if layer == 1:
            held["back"] = held["grads"], grads_of(1, held["grads"])
        q = after(q, hidden)
        heads, exact, lse = attend(meta, q, kvs)
        saved = (unit, scale, normed, attend_in, feed_in, q, kvs, heads, exact, lse, hidden, slope)
        if layer == 1:
            return None, saved
        partial = after(branch_of(0, heads, hidden), held["grads"])
        return stream + (scatter_near(scatter_far(partial)) + vec[4]), saved

    def reduce_rows(mats):
        mats = jnp.stack(mats)
        kept = pick(mats[:, :, :128], mats[:, :, 128:])
        other = swap(pick(mats[:, :, 128:], mats[:, :, :128]).astype(bf16))
        return (kept + other.astype(f32)).astype(bf16)

    def scatter_row(total):
        return lax.psum_scatter(total, "row", scatter_dimension=1, tiled=True).astype(f32)

    def backward(layer, grad_out, saved):
        unit, scale, normed, attend_in, feed_in, q, kvs, heads, exact, lse, hidden, slope = saved
        vec = vector_sets[layer]
        mixed, (expand, shrink) = whole_mixed[layer], whole_feed[layer]
        branch = grad_out.astype(bf16)
        if layer == 0:
            grads = gather_col(branch)
            grad_heads = grads_of(0, grads)
            grad_heads = after(grad_heads, held["last"])
        else:
            grads, grad_heads = held["back"]
            partial = branch_of(1, heads, hidden)
            held["plane"] = scatter_far(partial)
            held["last"] = scatter_near(held["plane"])
            grad_heads = after(grad_heads, partial)
        dq, d0, d1, d2 = attend_back(meta, q, kvs, grad_heads, exact, lse)
        got1, got2 = row_shift(d1, -1), row_shift(d2, -2)
        grad_pre = [(contract(grads[j], shrink, 1, 0) * slope[j]).astype(bf16) for j in range(4)]
        grads_all, grad_pre_all = jnp.concatenate(grads), jnp.concatenate(grad_pre)
        d_out = contract(grads_all, heads, 0, 0)
        d_shrink = contract(grads_all, jnp.concatenate(hidden), 0, 0)
        d_expand = contract(jnp.concatenate(feed_in), grad_pre_all, 0, 0)
        feed_total = reduce_rows([d_expand, d_shrink])
        dkv = d0.astype(f32) + got1.astype(f32) + got2.astype(f32)
        grad_joint = jnp.concatenate(
            [turn(dq, cosine, -sine), turn(dkv, cosine, -sine)], axis=1
        ).astype(bf16)
        grad_joint = after(grad_joint, feed_total)
        if layer == 1:
            grad_joint = after(grad_joint, held["plane"])
        chunks, parts = [None] * 4, []
        for j in (2, 1, 3, 0):
            chunks[j], sums = back_project(
                piece(grad_joint, j), grad_pre[j], mixed, expand, vec[0:1], vec[2:3], normed[j]
            )
            parts.append(sums)
        got = far_pieces(chunks)
        summed = scatter_near(far_sum(chunks, got))
        d_in = contract(attend_in, after(grad_joint, chunks), 0, 0)
        mixed_total = reduce_rows([d_in + jnp.pad(d_out, ((0, 0), (0, 2 * HD)))])
        smalls = jnp.concatenate(
            [
                sum(parts),
                jnp.sum(branch.astype(f32), axis=0, keepdims=True),
                jnp.concatenate(
                    [
                        jnp.sum(grad_joint.astype(f32), axis=0, keepdims=True),
                        jnp.sum(grad_pre_all.astype(f32), axis=0, keepdims=True),
                        jnp.zeros((1, 512), f32),
                    ],
                    axis=1,
                ),
            ]
        )
        smalls = after(smalls, got[0])
        inner = (
            summed
            - jnp.mean(summed, axis=-1, keepdims=True)
            - unit * jnp.mean(summed * unit, axis=-1, keepdims=True)
        )
        matrices = scatter_row(jnp.concatenate([mixed_total, feed_total]))
        return grad_out + inner * scale, matrices, smalls

    middle, saved0 = forward(0, stream0)
    _, saved1 = forward(1, middle)
    middle_grad, matrices1, smalls1 = backward(1, pick(cotangent[0], cotangent[1]), saved1)
    input_grad, matrices0, smalls0 = backward(0, middle_grad, saved0)
    last = middle + (held["last"] + vector_sets[1][4])

    def settle(of_first, of_second):
        return pick(of_first, of_second), swap(pick(of_second, of_first))

    kept, other = settle(matrices0, matrices1)
    matrices = jnp.concatenate([pick(kept, other), pick(other, kept)], axis=2)

    kept, other = settle(smalls0, smalls1)
    sums = kept + other
    sums = pair_sum(sums, "row", 1, 4)
    biases, sums = sums[5], sums[:5]
    sums = pair_sum(pair_sum(sums, "col", 1, 16), "col", 4, 16)

    def by_batch(of_first, of_second):
        kept, other = settle(of_first, of_second)
        return pick(jnp.stack([kept, other]), jnp.stack([other, kept]))[None]

    packed = matrices[0]
    return (
        by_batch(middle, last),
        by_batch(input_grad, middle_grad),
        jnp.concatenate([packed[:, :HD], packed[:, 2 * HD :]], axis=1)[None],
        jnp.concatenate([biases[:HD], biases[2 * HD : 256]])[None],
        packed[:, HD : 2 * HD].T[None],
        matrices[1][None],
        biases[256:512][None],
        matrices[2].T[None],
        sums[4][None],
        sums[0][None],
        sums[1][None],
        sums[2][None],
        sums[3][None],
    )


def solution(mesh):
    return jax.shard_map(
        on_device,
        mesh=mesh,
        in_specs=(
            P(None, ("row", "col"), None),
            P(None, ("row", "col"), None),
            P(),
            P("section", "row", "col"),
            P("section", "col"),
            P("section", "col", "row"),
            P("section", "row", "col"),
            P("section", "col"),
            P("section", "col", "row"),
            P("section", None),
            P("section", None),
            P("section", None),
            P("section", None),
            P("section", None),
        ),
        out_specs=(
            P("section", None, ("row", "col"), None),
            P("section", None, ("row", "col"), None),
            P("section", "row", "col"),
            P("section", "col"),
            P("section", "col", "row"),
            P("section", "row", "col"),
            P("section", "col"),
            P("section", "col", "row"),
            P("section", None),
            P("section", None),
            P("section", None),
            P("section", None),
            P("section", None),
        ),
        check_vma=False,
    )
```

```python
import functools
import math

import jax
import jax.numpy as jnp
from jax import lax
from jax.experimental import pallas as pl
from jax.experimental.pallas import tpu as pltpu
from jax.sharding import PartitionSpec as P

D = 1024
HD = 64
ROT = 16
EPSILON = 1e-05
BLOCK = 64
GROUP = 1024
WINDOW = 3
TQ = 256
TK = 512
LOW = -1e30

bf16 = jnp.bfloat16
f32 = jnp.float32


def col_pairs(stage, by):
    pairs = []
    for core in range(2):
        along_y = (stage == 1) == (core == 0)
        for z in range(4):
            for y in range(4):
                to = (z * 4 + (y + by) % 4) if along_y else (((z + by) % 4) * 4 + y)
                pairs.append((core * 16 + z * 4 + y, core * 16 + to))
    return pairs


def col_shift(value, stage, by):
    return lax.ppermute(value, ("section", "col"), col_pairs(stage, by))


def row_shift(value, by):
    return lax.ppermute(value, "row", [(i, (i + by) % 4) for i in range(4)])


def swap(value):
    return lax.ppermute(value, "section", [(0, 1), (1, 0)])


def gather_near(rows):
    return jnp.concatenate([rows] + [col_shift(rows, 1, k) for k in (1, 2, 3)], axis=0)


def gather_far(plane):
    return [plane] + [col_shift(plane, 2, k) for k in (1, 2, 3)]


def gather_col(rows):
    return gather_far(gather_near(rows))


def scatter_far(chunks):
    return far_sum(chunks, far_pieces(chunks))


def far_pieces(chunks):
    return [col_shift(chunks[k], 2, -k) for k in (1, 2, 3)]


def far_sum(chunks, got):
    return chunks[0].astype(f32) + sum(piece.astype(f32) for piece in got)


def scatter_near(plane):
    plane = plane.reshape(4, BLOCK, D)
    got = [col_shift(plane[k].astype(bf16), 1, -k) for k in (1, 2, 3)]
    return plane[0] + sum(piece.astype(f32) for piece in got)


def contract(left_side, right_side, left_dim, right_dim):
    return lax.dot_general(
        left_side,
        right_side,
        (((left_dim,), (right_dim,)), ((), ())),
        preferred_element_type=f32,
    )


def first_key(token, meta):
    start = jnp.zeros_like(token)
    end = 0
    for index in range(4):
        end = end + meta[index]
        start = jnp.where(token >= end, end, start)
    return start


def tile_mask(meta, row, low_token, key_token):
    query_token = low_token + lax.broadcasted_iota(jnp.int32, (TQ, 1), 0)
    start = first_key(query_token, meta)
    keys = key_token + lax.broadcasted_iota(jnp.int32, (1, TK), 1)
    return (keys >= start) & (keys <= query_token)


def to_order(meta, source, target, groups):
    for block in range(16):
        place = pl.multiple_of(meta[8 + block] * BLOCK, BLOCK)
        for from_group, to_group in groups:
            target[pl.ds(to_group * GROUP + place, BLOCK), :] = source[
                from_group * GROUP + block * BLOCK : from_group * GROUP + (block + 1) * BLOCK, :
            ]


def key_range(meta, row, tile):
    low_token = row * GROUP + tile * TQ
    base = (row - 2) * GROUP
    lowest = (first_key(low_token, meta) - base) // TK
    highest = (2 * GROUP + tile * TQ + TQ - 1) // TK
    return low_token, base, lowest, highest + 1


def attend_kernel(meta, q_ref, k0_ref, k1_ref, k2_ref, out_ref, exact_ref, lse_ref, q_s, kv_s, o_s):
    row = meta[4]
    to_order(meta, q_ref, q_s, [(0, 0)])
    for group, ref in ((0, k2_ref), (1, k1_ref), (2, k0_ref)):
        to_order(meta, ref, kv_s, [(0, group)])
    upper = lax.broadcasted_iota(jnp.int32, (TQ, 2 * HD), 1) >= HD

    def per_tile(tile, carry):
        rows = pl.ds(pl.multiple_of(tile * TQ, TQ), TQ)
        query = q_s[rows, :]
        low_token, base, lowest, highest = key_range(meta, row, tile)

        def step(index, state):
            top, total, acc = state
            kv = kv_s[pl.ds(pl.multiple_of(index * TK, TK), TK), :]
            scores = contract(query, kv, 1, 1)
            mask = tile_mask(meta, row, low_token, base + index * TK)
            scores = jnp.where(mask, scores, LOW)
            new_top = jnp.maximum(top, jnp.max(scores, axis=1, keepdims=True))
            weight = jnp.exp(scores - new_top)
            shrink = jnp.exp(top - new_top)
            total = total * shrink + jnp.sum(weight, axis=1, keepdims=True)
            acc = acc * shrink + contract(weight.astype(bf16), kv, 1, 0)
            return new_top, total, acc

        top, total, acc = lax.fori_loop(
            lowest,
            highest,
            step,
            (
                jnp.full((TQ, 1), LOW, f32),
                jnp.zeros((TQ, 1), f32),
                jnp.zeros((TQ, 2 * HD), f32),
            ),
        )
        exact = jnp.where(upper, acc / total, 0.0)
        exact_ref[rows, :] = exact
        o_s[rows, :] = exact.astype(bf16)
        lse_ref[rows, :] = top + jnp.log(total)
        return carry

    lax.fori_loop(0, GROUP // TQ, per_tile, 0)
    for block in range(16):
        place = pl.multiple_of(meta[8 + block] * BLOCK, BLOCK)
        out_ref[block * BLOCK : (block + 1) * BLOCK, :] = o_s[pl.ds(place, BLOCK), :]


def attend_back_kernel(
    meta, q_ref, k0_ref, k1_ref, k2_ref, g_ref, exact_ref, lse_ref,
    dq_ref, d0_ref, d1_ref, d2_ref, q_s, kv_s, g_s, dq_s, dkv_s,
):
    row = meta[4]
    to_order(meta, q_ref, q_s, [(0, 0)])
    to_order(meta, g_ref, g_s, [(0, 0)])
    for group, ref in ((0, k2_ref), (1, k1_ref), (2, k0_ref)):
        to_order(meta, ref, kv_s, [(0, group)])
    dkv_s[...] = jnp.zeros_like(dkv_s)

    def per_tile(tile, carry):
        rows = pl.ds(pl.multiple_of(tile * TQ, TQ), TQ)
        query = q_s[rows, :]
        grad = g_s[rows, :]
        lse = lse_ref[rows, :]
        delta = jnp.sum(grad.astype(f32) * exact_ref[rows, :], axis=1, keepdims=True)
        low_token, base, lowest, highest = key_range(meta, row, tile)

        def step(index, dq):
            keys = pl.ds(pl.multiple_of(index * TK, TK), TK)
            kv = kv_s[keys, :]
            scores = contract(query, kv, 1, 1)
            mask = tile_mask(meta, row, low_token, base + index * TK)
            probs = jnp.exp(jnp.where(mask, scores, LOW) - lse)
            grad_probs = contract(grad, kv, 1, 1)
            grad_scores = (probs * (grad_probs - delta)).astype(bf16)
            dkv_s[keys, :] += contract(grad_scores, query, 0, 0) + contract(
                probs.astype(bf16), grad, 0, 0
            )
            return dq + contract(grad_scores, kv, 1, 0)

        dq_s[rows, :] = lax.fori_loop(lowest, highest, step, jnp.zeros((TQ, 2 * HD), f32))
        return carry

    lax.fori_loop(0, GROUP // TQ, per_tile, 0)
    lower = lax.broadcasted_iota(jnp.int32, (BLOCK, 2 * HD), 1) < HD
    for block in range(16):
        place = pl.multiple_of(meta[8 + block] * BLOCK, BLOCK)
        here = slice(block * BLOCK, (block + 1) * BLOCK)
        dq_ref[here, :] = jnp.where(lower, dq_s[pl.ds(place, BLOCK), :] * (1.0 / math.sqrt(HD)), 0.0)
        for group, ref in ((0, d2_ref), (1, d1_ref), (2, d0_ref)):
            ref[here, :] = dkv_s[pl.ds(group * GROUP + place, BLOCK), :].astype(bf16)


VMEM = pl.BlockSpec(memory_space=pltpu.VMEM)
SMEM = pl.BlockSpec(memory_space=pltpu.SMEM)


def attend(meta, q, kvs):
    wide = (GROUP, 2 * HD)
    return pl.pallas_call(
        attend_kernel,
        out_shape=(
            jax.ShapeDtypeStruct(wide, bf16),
            jax.ShapeDtypeStruct(wide, f32),
            jax.ShapeDtypeStruct((GROUP, 1), f32),
        ),
        in_specs=[SMEM] + [VMEM] * 4,
        out_specs=(VMEM,) * 3,
        scratch_shapes=[
            pltpu.VMEM(wide, bf16),
            pltpu.VMEM((WINDOW * GROUP, 2 * HD), bf16),
            pltpu.VMEM(wide, bf16),
        ],
        compiler_params=pltpu.CompilerParams(vmem_limit_bytes=24 * 2**20),
        cost_estimate=pl.CostEstimate(
            flops=2_000_000_000, bytes_accessed=3_000_000, transcendentals=2_000_000
        ),
        name="attend",
    )(meta, q, *kvs)


def attend_back(meta, q, kvs, grad, exact, lse):
    wide = (GROUP, 2 * HD)
    return pl.pallas_call(
        attend_back_kernel,
        out_shape=(jax.ShapeDtypeStruct(wide, f32),) + (jax.ShapeDtypeStruct(wide, bf16),) * 3,
        in_specs=[SMEM] + [VMEM] * 7,
        out_specs=(VMEM,) * 4,
        scratch_shapes=[
            pltpu.VMEM(wide, bf16),
            pltpu.VMEM((WINDOW * GROUP, 2 * HD), bf16),
            pltpu.VMEM(wide, bf16),
            pltpu.VMEM(wide, f32),
            pltpu.VMEM((WINDOW * GROUP, 2 * HD), f32),
        ],
        compiler_params=pltpu.CompilerParams(vmem_limit_bytes=24 * 2**20),
        cost_estimate=pl.CostEstimate(
            flops=5_000_000_000, bytes_accessed=5_000_000, transcendentals=2_000_000
        ),
        name="attend_back",
    )(meta, q, *kvs, grad, exact, lse)


def after(value, *others):
    return lax.optimization_barrier((value,) + others)[0]


def turn_lanes(value, cosine, sine):
    lane = lax.broadcasted_iota(jnp.int32, value.shape, 1)
    swapped = jnp.where(
        lane < ROT // 2,
        pltpu.roll(value, 2 * HD - ROT // 2, 1),
        pltpu.roll(value, ROT // 2, 1),
    )
    return value * cosine + swapped * sine


def project_kernel(
    n0, n1, n2, n3, weight, bias, gain, shift, cosine, sine, attend_out, q_out, kv_out
):
    lower = lax.broadcasted_iota(jnp.int32, (256, 2 * HD), 1) < HD
    for j, normed in enumerate((n0, n1, n2, n3)):
        rows = slice(j * 256, (j + 1) * 256)
        attend_in = (gain[...] * normed[...].astype(f32) + shift[...]).astype(bf16)
        attend_out[rows, :] = attend_in
        joint = contract(attend_in, weight[...], 1, 0) + bias[...]
        c, s = cosine[rows, :], sine[rows, :]
        q = turn_lanes(joint[:, : 2 * HD], c, s).astype(bf16).astype(f32)
        q_out[rows, :] = jnp.where(lower, q * (1.0 / math.sqrt(HD)), 0.0).astype(bf16)
        kv_out[rows, :] = turn_lanes(joint[:, 2 * HD :], c, s).astype(bf16)


def project(normed, weight, bias, gain, shift, cosine, sine):
    wide = jax.ShapeDtypeStruct((GROUP, 2 * HD), bf16)
    return pl.pallas_call(
        project_kernel,
        out_shape=(jax.ShapeDtypeStruct((GROUP, D), bf16), wide, wide),
        in_specs=[VMEM] * 10,
        out_specs=(VMEM,) * 3,
        compiler_params=pltpu.CompilerParams(vmem_limit_bytes=24 * 2**20),
        cost_estimate=pl.CostEstimate(
            flops=2 * GROUP * D * 256, bytes_accessed=6 * 2**20, transcendentals=0
        ),
        name="project",
    )(*normed, weight, bias, gain, shift, cosine, sine)


def back_kernel(gj, gp, mixed, expand, gain_a, gain_f, normed, out_ref, sums_ref):
    grad_attend = contract(gj[...], mixed[...], 1, 1)
    grad_feed = contract(gp[...], expand[...], 1, 1)
    out_ref[...] = (gain_a[...] * grad_attend + gain_f[...] * grad_feed).astype(bf16)
    wide = normed[...].astype(f32)
    sums_ref[0:1, :] = jnp.sum(wide * grad_attend, axis=0, keepdims=True)
    sums_ref[1:2, :] = jnp.sum(grad_attend, axis=0, keepdims=True)
    sums_ref[2:3, :] = jnp.sum(wide * grad_feed, axis=0, keepdims=True)
    sums_ref[3:4, :] = jnp.sum(grad_feed, axis=0, keepdims=True)


def back_project(gj, gp, mixed, expand, gain_a, gain_f, normed):
    return pl.pallas_call(
        back_kernel,
        out_shape=(
            jax.ShapeDtypeStruct((256, D), bf16),
            jax.ShapeDtypeStruct((4, D), f32),
        ),
        in_specs=[VMEM] * 7,
        out_specs=(VMEM,) * 2,
        compiler_params=pltpu.CompilerParams(vmem_limit_bytes=16 * 2**20),
        cost_estimate=pl.CostEstimate(
            flops=4 * 256 * D * 256, bytes_accessed=3 * 2**20, transcendentals=0
        ),
        name="back_project",
    )(gj, gp, mixed, expand, gain_a, gain_f, normed)


def pair_sum(value, axis, step, count):
    for flip in (1, 3):
        pairs = [(i, i + (((i // step) % 4 ^ flip) - (i // step) % 4) * step) for i in range(count)]
        value = value + lax.ppermute(value, axis, pairs)
    return value


def norm_parts(stream):
    center = stream - jnp.mean(stream, axis=-1, keepdims=True)
    spread = jnp.mean(center * center, axis=-1, keepdims=True)
    scale = lax.rsqrt(spread + EPSILON)
    return center * scale, scale


def turn_tables(position):
    half_turn = ROT // 2
    frequency = 10000.0 ** (-(jnp.arange(half_turn, dtype=f32) * 2.0) / ROT)
    angles = position.astype(f32)[:, None] * jnp.concatenate([frequency, frequency])[None, :]
    sign = jnp.where(jnp.arange(ROT) < half_turn, -1.0, 1.0)
    rest = 2 * HD - ROT
    rows = position.shape[0]
    cosine = jnp.concatenate([jnp.cos(angles), jnp.ones((rows, rest), f32)], axis=1)
    sine = jnp.concatenate([jnp.sin(angles) * sign, jnp.zeros((rows, rest), f32)], axis=1)
    return cosine, sine


def turn(value, cosine, sine):
    half_turn = ROT // 2
    swapped = jnp.concatenate(
        [value[:, half_turn:ROT], value[:, :half_turn], value[:, ROT:]], axis=1
    )
    return value * cosine + swapped * sine


def on_device(
    tokens,
    cotangent,
    seq_lengths,
    attention_in,
    attention_in_bias,
    attention_out,
    expand_weight,
    expand_bias,
    shrink_weight,
    output_bias,
    attend_gain,
    attend_shift,
    feed_gain,
    feed_shift,
):
    row = lax.axis_index("row")
    col = lax.axis_index("col")
    section = lax.axis_index("section")
    first = section == 0
    pick = lambda a, b: jnp.where(first, a, b)

    stream0 = pick(tokens[0], tokens[1])
    unit0, scale0 = norm_parts(stream0)
    plane0 = gather_near(unit0.astype(bf16))
    chunks0 = gather_far(plane0)

    vectors = jnp.concatenate(
        [
            attend_gain,
            attend_shift,
            feed_gain,
            feed_shift,
            output_bias,
            jnp.concatenate(
                [
                    attention_in_bias[:, :HD],
                    jnp.zeros((1, HD), f32),
                    attention_in_bias[:, HD:],
                    expand_bias,
                    jnp.zeros((1, 512), f32),
                ],
                axis=1,
            ),
        ],
        axis=0,
    )
    their_vectors = swap(vectors)
    vector_sets = (pick(vectors, their_vectors), pick(their_vectors, vectors))

    lengths = pick(seq_lengths[0], seq_lengths[1])
    y, z = col % 4, col // 4
    near, far = pick(y, z), pick(z, y)
    block = jnp.arange(16)
    near_at, far_at = (near - block % 4) % 4, (far - block // 4) % 4
    places = pick(far_at * 4 + near_at, near_at * 4 + far_at)
    token = row * GROUP + (places[:, None] * BLOCK + jnp.arange(BLOCK)[None, :]).reshape(GROUP)
    position = token - first_key(token, after(lengths, plane0))
    cosine, sine = turn_tables(position)
    meta = jnp.concatenate(
        [lengths, row[None], jnp.zeros((3,), jnp.int32), places]
    ).astype(jnp.int32)

    piece = lambda value, j: value[j * 256 : (j + 1) * 256]

    own = attention_in[0]
    mixed = jnp.concatenate([own[:, :HD], attention_out[0].T, own[:, HD:]], axis=1)
    theirs = swap(mixed)
    mixed = after(jnp.stack([pick(mixed, theirs), pick(theirs, mixed)]), plane0)
    near = [mixed] + [row_shift(mixed, -k) for k in (1, 2, 3)]
    near = after(near, chunks0, cosine, sine)
    near = jnp.concatenate(near + near[:3], axis=1)
    near = lax.dynamic_slice(near, (0, ((4 - row) % 4) * 256, 0), (2, D, 256))
    whole_mixed = (near[0], near[1])
    mine = lax.all_gather(
        jnp.stack([expand_weight[0], shrink_weight[0].T]), "row", axis=1, tiled=True
    )
    theirs = swap(mine)
    whole_feed = (pick(mine, theirs), pick(theirs, mine))

    held = {}
    upper = (jnp.arange(2 * HD) >= HD)[None, :]

    def branch_of(layer, heads, hidden):
        out, shrink = whole_mixed[layer][:, : 2 * HD], whole_feed[layer][1]
        return [
            (contract(piece(heads, j), out, 1, 1) + contract(hidden[j], shrink, 1, 1)).astype(bf16)
            for j in range(4)
        ]

    def grads_of(layer, grads):
        out = whole_mixed[layer][:, : 2 * HD]
        return jnp.concatenate(
            [jnp.where(upper, contract(grads[j], out, 1, 0), 0.0).astype(bf16) for j in range(4)]
        )

    def forward(layer, stream):
        vec = vector_sets[layer]
        if layer == 0:
            unit, scale, normed = unit0, scale0, chunks0
        else:
            unit, scale = norm_parts(stream)
            normed = gather_col(unit.astype(bf16))
        attend_in, q, kv = project(
            normed, whole_mixed[layer], vec[5:6, :256], vec[0:1], vec[1:2], cosine, sine
        )
        kvs = (kv, row_shift(kv, 1), row_shift(kv, 2))
        if layer == 0:
            branch = pick(cotangent[0], cotangent[1]).astype(bf16)
            held["grads"] = gather_col(after(branch, chunks0))
        feed_in, hidden, slope = [], [], []
        for j in range(4):
            feed_in.append((vec[2] * normed[j] + vec[3]).astype(bf16))
            pre = contract(feed_in[j], whole_feed[layer][0], 1, 0) + vec[5, 256:512]
            cdf = 0.5 * (1.0 + lax.erf(pre * math.sqrt(0.5)))
            hidden.append((pre * cdf).astype(bf16))
            slope.append(cdf + pre * jnp.exp(-0.5 * pre * pre) * (1.0 / math.sqrt(2 * math.pi)))
        if layer == 1:
            held["back"] = held["grads"], grads_of(1, held["grads"])
        q = after(q, hidden)
        heads, exact, lse = attend(meta, q, kvs)
        saved = (unit, scale, normed, attend_in, feed_in, q, kvs, heads, exact, lse, hidden, slope)
        if layer == 1:
            return None, saved
        partial = after(branch_of(0, heads, hidden), held["grads"])
        return stream + (scatter_near(scatter_far(partial)) + vec[4]), saved

    def reduce_rows(mats):
        mats = jnp.stack(mats)
        kept = pick(mats[:, :, :128], mats[:, :, 128:])
        other = swap(pick(mats[:, :, 128:], mats[:, :, :128]).astype(bf16))
        return (kept + other.astype(f32)).astype(bf16)

    def scatter_row(total):
        return lax.psum_scatter(total, "row", scatter_dimension=1, tiled=True).astype(f32)

    def backward(layer, grad_out, saved):
        unit, scale, normed, attend_in, feed_in, q, kvs, heads, exact, lse, hidden, slope = saved
        vec = vector_sets[layer]
        mixed, (expand, shrink) = whole_mixed[layer], whole_feed[layer]
        branch = grad_out.astype(bf16)
        if layer == 0:
            near = gather_near(branch)
            grads = gather_far(near)
            held["last"] = scatter_near(after(held["plane"], near))
            grad_heads = after(grads_of(0, grads), held["last"])
        else:
            grads, grad_heads = held["back"]
            partial = branch_of(1, heads, hidden)
            held["plane"] = scatter_far(partial)
            grad_heads = after(grad_heads, partial)
        dq, d0, d1, d2 = attend_back(meta, q, kvs, grad_heads, exact, lse)
        got1, got2 = row_shift(d1, -1), row_shift(d2, -2)
        grad_pre = [(contract(grads[j], shrink, 1, 0) * slope[j]).astype(bf16) for j in range(4)]
        grads_all, grad_pre_all = jnp.concatenate(grads), jnp.concatenate(grad_pre)
        d_out = contract(grads_all, heads, 0, 0)
        d_shrink = contract(grads_all, jnp.concatenate(hidden), 0, 0)
        d_expand = contract(jnp.concatenate(feed_in), grad_pre_all, 0, 0)
        feed_total = reduce_rows([d_expand, d_shrink])
        dkv = d0.astype(f32) + got1.astype(f32) + got2.astype(f32)
        grad_joint = jnp.concatenate(
            [turn(dq, cosine, -sine), turn(dkv, cosine, -sine)], axis=1
        ).astype(bf16)
        grad_joint = after(grad_joint, feed_total)
        if layer == 1:
            grad_joint = after(grad_joint, held["plane"])
        chunks, parts = [None] * 4, []
        for j in (2, 1, 3, 0):
            chunks[j], sums = back_project(
                piece(grad_joint, j), grad_pre[j], mixed, expand, vec[0:1], vec[2:3], normed[j]
            )
            parts.append(sums)
        got = far_pieces(chunks)
        summed = scatter_near(far_sum(chunks, got))
        d_in = contract(attend_in, after(grad_joint, chunks), 0, 0)
        mixed_total = reduce_rows([d_in + jnp.pad(d_out, ((0, 0), (0, 2 * HD)))])
        smalls = jnp.concatenate(
            [
                sum(parts),
                jnp.sum(branch.astype(f32), axis=0, keepdims=True),
                jnp.concatenate(
                    [
                        jnp.sum(grad_joint.astype(f32), axis=0, keepdims=True),
                        jnp.sum(grad_pre_all.astype(f32), axis=0, keepdims=True),
                        jnp.zeros((1, 512), f32),
                    ],
                    axis=1,
                ),
            ]
        )
        smalls = after(smalls, got[2])
        inner = (
            summed
            - jnp.mean(summed, axis=-1, keepdims=True)
            - unit * jnp.mean(summed * unit, axis=-1, keepdims=True)
        )
        matrices = scatter_row(jnp.concatenate([mixed_total, feed_total]))
        return grad_out + inner * scale, matrices, smalls

    middle, saved0 = forward(0, stream0)
    _, saved1 = forward(1, middle)
    middle_grad, matrices1, smalls1 = backward(1, pick(cotangent[0], cotangent[1]), saved1)
    input_grad, matrices0, smalls0 = backward(0, middle_grad, saved0)
    last = middle + (held["last"] + vector_sets[1][4])

    def settle(of_first, of_second):
        return pick(of_first, of_second), swap(pick(of_second, of_first))

    kept, other = settle(matrices0, matrices1)
    matrices = jnp.concatenate([pick(kept, other), pick(other, kept)], axis=2)

    kept, other = settle(smalls0, smalls1)
    sums = kept + other
    sums = pair_sum(sums, "row", 1, 4)
    biases, sums = sums[5], sums[:5]
    sums = pair_sum(pair_sum(sums, "col", 1, 16), "col", 4, 16)

    def by_batch(of_first, of_second):
        kept, other = settle(of_first, of_second)
        return pick(jnp.stack([kept, other]), jnp.stack([other, kept]))[None]

    packed = matrices[0]
    return (
        by_batch(middle, last),
        by_batch(input_grad, middle_grad),
        jnp.concatenate([packed[:, :HD], packed[:, 2 * HD :]], axis=1)[None],
        jnp.concatenate([biases[:HD], biases[2 * HD : 256]])[None],
        packed[:, HD : 2 * HD].T[None],
        matrices[1][None],
        biases[256:512][None],
        matrices[2].T[None],
        sums[4][None],
        sums[0][None],
        sums[1][None],
        sums[2][None],
        sums[3][None],
    )


def solution(mesh):
    return jax.shard_map(
        on_device,
        mesh=mesh,
        in_specs=(
            P(None, ("row", "col"), None),
            P(None, ("row", "col"), None),
            P(),
            P("section", "row", "col"),
            P("section", "col"),
            P("section", "col", "row"),
            P("section", "row", "col"),
            P("section", "col"),
            P("section", "col", "row"),
            P("section", None),
            P("section", None),
            P("section", None),
            P("section", None),
            P("section", None),
        ),
        out_specs=(
            P("section", None, ("row", "col"), None),
            P("section", None, ("row", "col"), None),
            P("section", "row", "col"),
            P("section", "col"),
            P("section", "col", "row"),
            P("section", "row", "col"),
            P("section", "col"),
            P("section", "col", "row"),
            P("section", None),
            P("section", None),
            P("section", None),
            P("section", None),
            P("section", None),
        ),
        check_vma=False,
    )
```
